32 devices in a mesh: shot: 4 (over x, core), cmp: 8 (over z, y).
Axes of the slice: x: 2, y: 2, z: 4, core: 2. Of those that a mesh axis runs over, the one named last changes fastest.
Arguments:
- traces: float32 [4096, 1920], P(('shot', 'cmp')), may hold values from -6 to 6
- statics: int32 [4096], P(('shot', 'cmp')), may hold values from -24 to 24
- cmp_owner: int32 [4096, 1], P(('shot', 'cmp')), may hold values from 0 to 31; in each aligned block of 128 rows (0 to 127, 128 to 255, ...) at most 8 rows name the same one
- cmp_offset: int32 [4096], P(('shot', 'cmp')), may hold values from 0 to 31
- shot_id: int32 [4096], P(('shot', 'cmp')), may hold values from 0 to 511, as said below
- receiver_id: int32 [4096], P(('shot', 'cmp')), may hold values from 0 to 511
Outputs:
- source_corr: float32 [512, 128], P(('shot', 'cmp'))
- receiver_corr: float32 [512, 128], P(('shot', 'cmp'))
The draws below stay inside these ranges and needn't reach their ends.
Inputs may be any that keep to these rules, and one draw needn't show every extreme that they name: `cmp_owner`: in the 128 traces of one device (aligned blocks of the trace dimension), no owner is named by more than 8 traces. `shot_id`: the traces of block k of 128 traces come from shots k * 16 to (k + 1) * 16 - 1.
All inputs are finite; a program needn't handle non-finite values.
Results may differ from the reference program's by a relative error of at most 0.000078.
Values sent between devices are 32-bit elements; how exact they have to be, the bound alone decides.
A program may use at most 128 MiB of HBM per device.

```python
import math
import jax
import jax.numpy as jnp
import numpy as np
from jax import lax

NS = 1920
LAGS = 128
MAX_SHIFT = 24
TR_DEV = 128
CMP_DEV = 32
SHOT_DEV = 16
TRACES = 4096
CMPS = 1024
SOURCES = 512
RECEIVERS = 512
CAP = 8
DEVICES = 32


def draw_shot_id(key, part):
    key = jax.random.fold_in(key, 5)
    positions = jnp.arange(TRACES, dtype=jnp.int32)
    within = jax.random.randint(key, (TRACES,), 0, SHOT_DEV, dtype=jnp.int32)
    return positions // TR_DEV * SHOT_DEV + within


def with_ends(entries, rng, low, high):
    dims = entries.shape
    spot = [jax.random.randint(jax.random.fold_in(rng, axis), (), 0, dims[axis]) for axis in range(len(dims))]
    entries = entries.at[tuple(spot)].set(low)
    longest = dims.index(max(dims))
    spot[longest] = (spot[longest] + 1) % dims[longest]
    return entries.at[tuple(spot)].set(high)


def steps_of(rng, shape, cuts, smallest, largest):
    def one(axis_at, blocks):
        steps = jax.random.uniform(jax.random.fold_in(jax.random.fold_in(rng, 6), axis_at), (blocks,), jnp.float32, smallest / len(cuts), largest / len(cuts))
        return jnp.repeat(jnp.exp(steps), shape[axis_at] // blocks).reshape((-1,) + (1,) * (len(shape) - axis_at - 1))

    loudness = one(*cuts[0])
    for cut in cuts[1:]:
        loudness = loudness * one(*cut)
    return loudness


def deal_out(rng, own, number, rows, number_of, top, most, skew):
    ranking = jax.random.permutation(rng, number_of)
    heavy_load, usual = portions_of(number_of, rows * top, most, skew, True), portions_of(number_of, rows * top, most, skew, False)
    places = jnp.arange(number_of)

    def named(sizes, turn):
        used = int((sizes > 0).sum())
        fixed = max(1, used // 4)
        moved = fixed + (places - fixed + turn * (used - fixed)) % max(1, number_of - fixed)
        return jnp.zeros((number_of,), jnp.int32).at[ranking[jnp.where(places < fixed, places, moved)]].set(jnp.asarray(sizes, jnp.int32))

    sizes = jnp.where(number % 4 == 0, named(heavy_load, number // 4), named(usual, number - number // 4 - 1))
    mixed = jax.random.permutation(jax.random.fold_in(own, 3), number_of)
    giver, receiver = mixed[0:number_of // 2 * 2:2], mixed[1:number_of // 2 * 2:2]
    room = jnp.minimum(sizes[giver] - 1, most - sizes[receiver]) // 2
    room = jnp.where((giver == ranking[0]) | (receiver == ranking[0]) | (sizes[receiver] == 0), 0, jnp.maximum(room, 0))
    moved = jax.random.randint(jax.random.fold_in(own, 4), (number_of // 2,), 0, 1 << 20) % (room + 1)
    sizes = sizes.at[giver].add(-moved).at[receiver].add(moved)
    labels = jnp.searchsorted(jnp.cumsum(sizes), jnp.arange(rows * top), side="right").astype(jnp.int32)
    grid = labels.reshape(top, rows).T
    grid = grid[jax.random.permutation(jax.random.fold_in(own, 1), rows)]
    turn = jax.random.randint(jax.random.fold_in(own, 2), (rows, 1), 0, top)
    return jnp.take_along_axis(grid, (jnp.arange(top)[None, :] + turn) % top, axis=1)


def portions_of(number_of, total, reach, lean, full):
    portions = [(1 << 20) // math.isqrt(standing ** lean) + 1 for standing in range(1, number_of + 1)]
    largest = reach if full else min(reach, max(-(-total // number_of), total * portions[0] // sum(portions)))
    least = 1 if total - largest >= number_of - 1 else 0
    counts, surplus = [largest] + [least] * (number_of - 1), total - largest - least * (number_of - 1)
    while surplus > 0:
        free = [i for i in range(1, number_of) if counts[i] < largest] or [i for i in range(1, number_of) if counts[i] < reach]
        whole, left = sum([portions[i] for i in free]), surplus
        for i in free:
            more = min(reach - counts[i], max(1, left * portions[i] // whole), surplus)
            counts[i] = counts[i] + more
            surplus = surplus - more
    return np.array(counts)


def scatter_about(rng, extent, spread, reach, split=(), kind=jnp.bfloat16):
    array = jax.random.normal(rng, extent, jnp.float32) * spread
    if len(split) > 0:
        array = steps_of(rng, extent, split, -0.22, 0.18) * array
    return jnp.clip(array, min=-reach, max=reach).astype(kind)


def setup_inputs(seed: int = 0) -> dict:
    key_list = jax.random.split(jax.random.key(seed), 7)
    traces = scatter_about(key_list[0], (TRACES, NS), 1.0, 6.0, ((0, 32),), jnp.float32)
    statics = with_ends(jax.random.randint(key_list[1], (TRACES,), 0 - MAX_SHIFT, MAX_SHIFT + 1), jax.random.fold_in(key_list[1], 1), 0 - MAX_SHIFT, MAX_SHIFT).astype(jnp.int32)
    cmp_owner_keys = jax.random.split(jax.random.fold_in(key_list[2], 1), TRACES // TR_DEV)
    cmp_owner_turns = jax.random.permutation(jax.random.fold_in(key_list[2], 3), TRACES // TR_DEV)
    cmp_owner = jax.vmap(lambda own, number: deal_out(jax.random.fold_in(key_list[2], 2), own, number, TR_DEV, DEVICES, 1, CAP, 2))(cmp_owner_keys, cmp_owner_turns).reshape((TRACES, 1))
    cmp_offset = with_ends(jax.random.randint(key_list[3], (TRACES,), 0, CMP_DEV), jax.random.fold_in(key_list[3], 1), 0, CMP_DEV - 1).astype(jnp.int32)
    shot_id = draw_shot_id(jax.random.fold_in(key_list[6], 71), 0)
    receiver_id = with_ends(jax.random.randint(key_list[5], (TRACES,), 0, RECEIVERS), jax.random.fold_in(key_list[5], 1), 0, RECEIVERS - 1).astype(jnp.int32)
    return {"traces": traces, "statics": statics, "cmp_owner": cmp_owner, "cmp_offset": cmp_offset, "shot_id": shot_id, "receiver_id": receiver_id}


stack_scale = 0.125


def shift_traces(traces, statics):
    padded = jnp.pad(traces, ((0, 0), (MAX_SHIFT, MAX_SHIFT)))
    starts = (MAX_SHIFT - statics).astype(jnp.int32)
    width = traces.shape[1]
    return jax.vmap(lambda row, first: lax.dynamic_slice_in_dim(row, first, width))(padded, starts)


def reference(traces, statics, cmp_owner, cmp_offset, shot_id, receiver_id):
    shifted = shift_traces(traces, statics)
    bins = (cmp_owner[:, 0] * CMP_DEV + cmp_offset).astype(jnp.int32)
    pilots = jax.ops.segment_sum(shifted, bins, num_segments=CMPS)
    padded = jnp.pad(pilots, ((0, 0), (LAGS // 2, LAGS // 2)))
    length = NS + LAGS
    pilot_spectra = jnp.fft.rfft(padded, axis=1)

    def one_block(block_start):
        rows_here = lax.dynamic_slice_in_dim(shifted, block_start, TR_DEV)
        bins_here = lax.dynamic_slice_in_dim(bins, block_start, TR_DEV)
        trace_spectra = jnp.fft.rfft(rows_here, n=length, axis=1)
        product = jnp.conj(trace_spectra) * pilot_spectra[bins_here]
        return jnp.fft.irfft(product, n=length, axis=1)[:, :LAGS]

    block_starts = jnp.arange(DEVICES, dtype=jnp.int32) * TR_DEV
    lagged = lax.map(one_block, block_starts).reshape(TRACES, LAGS) / NS
    source_corr = jax.ops.segment_sum(lagged, shot_id, num_segments=SOURCES) * stack_scale
    receiver_corr = jax.ops.segment_sum(lagged, receiver_id, num_segments=RECEIVERS) * stack_scale
    return (source_corr, receiver_corr)
```

```python
import functools

import jax
import jax.numpy as jnp
import ml_dtypes
import numpy as np
from jax import lax
from jax.experimental import pallas as pl
from jax.experimental.pallas import tpu as pltpu
from jax.sharding import PartitionSpec as P

LAGS = 128
MAX_SHIFT = 24
CMP_DEV = 32
SHOT_DEV = 16
REC_DEV = 16
BLOCK = 128
STACK_SCALE = 0.125

f32 = jnp.float32
bf16 = jnp.bfloat16
MESH = pl.DeviceIdType.MESH


def transform_tables(sample_total):
    u = np.arange(BLOCK)[:, None]
    f = np.arange(BLOCK)[None, :]
    angle = 2 * np.pi * ((u * f) % 256) / 256
    imag = -np.sin(angle)
    imag[:, 0] = 1 - 2 * (np.arange(BLOCK) % 2)
    forward = np.concatenate([np.cos(angle), imag], axis=1)
    weight = np.full((BLOCK, 1), 2.0)
    weight[0] = 1
    back_imag = -2 * np.sin(angle)
    back_imag[0] = 1 - 2 * (np.arange(BLOCK) % 2)
    inverse = np.concatenate([weight * np.cos(angle), back_imag], axis=0)
    inverse = inverse / 256 / sample_total * STACK_SCALE
    tables = []
    for table in (forward, inverse):
        high = table.astype(ml_dtypes.bfloat16)
        low = (table - high.astype(np.float64)).astype(ml_dtypes.bfloat16)
        tables += [high, low]
    return tables


def halves(x):
    high = x.astype(bf16)
    return high, (x - high.astype(f32)).astype(bf16)


def mm(a, b):
    return jnp.dot(a, b, preferred_element_type=f32)


def mm_nt(a, b):
    return lax.dot_general(a, b, (((1,), (1,)), ((), ())), preferred_element_type=f32)


def mm3(a, b_high, b_low):
    high, low = halves(a)
    return mm(high, b_high) + mm(low, b_high) + mm(high, b_low)


def iota(shape, dim):
    return lax.broadcasted_iota(jnp.int32, shape, dim)


def onehot(mask):
    return jnp.where(mask, 1.0, 0.0).astype(bf16)


def exact_dot(a, b):
    return jnp.dot(a, b, precision=lax.Precision.HIGHEST, preferred_element_type=f32)


def kernel(
    n, n_cmp, cap,
    owner_ref, offset_ref, shot_ref, receiver_ref, statics_ref, traces_ref,
    fwd_high_ref, fwd_low_ref, inv_high_ref, inv_low_ref,
    source_ref, received_ref,
    shifted, outbox, inbox, label_rows, label_out, label_in, spectra, corr, lag_out, lag_in, rec_out, rec_in,
    send_sem, recv_sem,
):
    rows = n * cap
    traces, samples = traces_ref.shape
    blocks = samples // BLOCK
    me = lax.axis_index("shot") * n_cmp + lax.axis_index("cmp")

    def place(d):
        return (d // n_cmp, lax.rem(d, n_cmp))

    barrier = pltpu.get_barrier_semaphore()

    @pl.loop(1, n)
    def _(k):
        pl.semaphore_signal(barrier, inc=1, device_id=place(lax.rem(me + k, n)), device_id_type=MESH)

    def trace_copy(d, slot):
        return pltpu.make_async_remote_copy(
            src_ref=outbox.at[pl.ds(pl.multiple_of(d * cap, 8), cap)],
            dst_ref=inbox.at[pl.ds(pl.multiple_of(slot * cap, 8), cap)],
            send_sem=send_sem.at[0, d], recv_sem=recv_sem.at[0, slot], device_id=place(d), device_id_type=MESH,
        )

    def label_copy(d, slot):
        return pltpu.make_async_remote_copy(
            src_ref=label_out.at[d], dst_ref=label_in.at[slot],
            send_sem=send_sem.at[1, d], recv_sem=recv_sem.at[1, slot], device_id=place(d), device_id_type=MESH,
        )

    def lag_copy(d, slot):
        return pltpu.make_async_remote_copy(
            src_ref=lag_out.at[pl.ds(pl.multiple_of(d * cap, 8), cap)],
            dst_ref=lag_in.at[pl.ds(pl.multiple_of(slot * cap, 8), cap)],
            send_sem=send_sem.at[2, d], recv_sem=recv_sem.at[2, slot], device_id=place(d), device_id_type=MESH,
        )

    def rec_copy(d, slot):
        return pltpu.make_async_remote_copy(
            src_ref=rec_out.at[pl.ds(pl.multiple_of(d * REC_DEV, 8), REC_DEV)],
            dst_ref=rec_in.at[pl.ds(pl.multiple_of(slot * REC_DEV, 8), REC_DEV)],
            send_sem=send_sem.at[3, d], recv_sem=recv_sem.at[3, slot], device_id=place(d), device_id_type=MESH,
        )

    statics_row = statics_ref[...]
    eye = iota((traces, traces), 0) == iota((traces, traces), 1)
    amount = jnp.sum(jnp.where(eye, statics_row, 0), axis=1, keepdims=True) + MAX_SHIFT
    step = 16
    for first in range(0, traces, step):
        row = jnp.concatenate([traces_ref[first : first + step, :], jnp.zeros((step, BLOCK), f32)], axis=1)
        width = samples + BLOCK
        here = amount[first : first + step]
        row = pltpu.roll(row, width - MAX_SHIFT, 1)
        for bit in range((2 * MAX_SHIFT).bit_length()):
            row = jnp.where((here >> bit) & 1 == 1, pltpu.roll(row, 1 << bit, 1), row)
        high, low = halves(row[:, :samples])
        shifted[first : first + step, :] = high
        shifted[traces + first : traces + first + step, :] = low

    owner = owner_ref[...]
    member = iota((n, traces), 0) == owner
    upper = onehot(iota((traces, traces), 0) <= iota((traces, traces), 1))
    counts = mm(onehot(member), upper)
    rank = jnp.sum(jnp.where(member, counts, 0.0), axis=0, keepdims=True).astype(jnp.int32) - 1
    target = owner * cap + rank
    put = onehot(iota((rows, traces), 0) == target)
    put_twice = jnp.concatenate([put, put], axis=1)
    for first in range(0, samples, 3 * BLOCK):
        outbox[:, first : first + 3 * BLOCK] = mm(put_twice, shifted[:, first : first + 3 * BLOCK])

    seat = iota((BLOCK, traces), 0)
    bins_here = jnp.where(member, (offset_ref[...] + 1).astype(f32), 0.0)
    rec_here = jnp.where(member, (receiver_ref[...] + 1).astype(f32), 0.0)

    def exact_nt(a, b):
        return lax.dot_general(
            a, b, (((1,), (1,)), ((), ())), precision=lax.Precision.HIGHEST, preferred_element_type=f32
        )

    label_rows[...] = exact_nt(bins_here, jnp.where(seat == rank, 1.0, 0.0)) + exact_nt(
        rec_here, jnp.where(seat == rank + 64, 1.0, 0.0)
    )

    @pl.loop(0, n)
    def _(d):
        label_out[d] = label_rows[pl.ds(d, 1), :]

    pl.semaphore_wait(barrier, n - 1)

    @pl.loop(1, n)
    def _(k):
        d = lax.rem(me + k, n)
        label_copy(d, me).start()
        trace_copy(d, me).start()

    mine = pl.ds(pl.multiple_of(me * cap, 8), cap)
    inbox[mine, :] = outbox[mine, :]
    label_in[me] = label_out[me]

    own_shot = onehot(iota((SHOT_DEV, traces), 0) == lax.rem(shot_ref[...], SHOT_DEV))
    take = mm_nt(own_shot, put).astype(bf16)

    @pl.loop(1, n)
    def _(k):
        d = lax.rem(me + (n - k), n)
        label_copy(d, d).wait_recv()
        trace_copy(d, d).wait_recv()

    @pl.loop(0, n)
    def _(d):
        label_rows[pl.ds(d, 1), :] = label_in[d]

    labels = label_rows[...]
    spread = jnp.where(iota((rows, n), 0) // cap == iota((rows, n), 1), 1.0, 0.0)
    slot_col = iota((rows, BLOCK), 0) % cap
    lane_col = iota((rows, BLOCK), 1)
    per_slot = exact_dot(spread, labels)
    bin_col = jnp.sum(jnp.where(slot_col == lane_col, per_slot, 0.0), axis=1, keepdims=True).astype(jnp.int32) - 1
    slot_row = iota((BLOCK, rows), 1) % cap
    lane_row = iota((BLOCK, rows), 0)
    mine_row = iota((n, rows), 1) // cap == iota((n, rows), 0)
    bin_all = exact_dot(labels, jnp.where(slot_row == lane_row, 1.0, 0.0))
    rec_all = exact_dot(labels, jnp.where(slot_row + 64 == lane_row, 1.0, 0.0))
    bin_row = jnp.sum(jnp.where(mine_row, bin_all, 0.0), axis=0, keepdims=True).astype(jnp.int32) - 1
    rec_row = jnp.sum(jnp.where(mine_row, rec_all, 0.0), axis=0, keepdims=True).astype(jnp.int32) - 1
    gather = onehot(iota((rows, CMP_DEV), 1) == bin_col)
    gather_twice = jnp.concatenate([gather, gather], axis=1)
    stack = onehot(iota((CMP_DEV, rows), 0) == bin_row)
    pick = onehot(iota((REC_DEV * n, rows), 0) == rec_row)

    pilots = []
    for j in range(blocks):
        high, low = halves(inbox[:, j * BLOCK : (j + 1) * BLOCK])
        pilots.append(mm(stack, high) + mm(stack, low))
    pilots.append(jnp.zeros((CMP_DEV, BLOCK), f32))
    moved = pltpu.roll(jnp.concatenate(pilots, axis=1), LAGS // 2, 1)
    fwd_high, fwd_low = fwd_high_ref[...], fwd_low_ref[...]
    for j in range(blocks + 1):
        spectra[j] = mm3(moved[:, j * BLOCK : (j + 1) * BLOCK], fwd_high, fwd_low)

    lane = iota((CMP_DEV, BLOCK), 1)
    turn = (1 - 2 * (iota((CMP_DEV, 2 * BLOCK), 1) % 2)).astype(f32)
    corr[...] = jnp.zeros_like(corr)

    @pl.loop(0, blocks)
    def _(j):
        window = spectra[j] + turn * spectra[j + 1]
        real, imag = window[:, :BLOCK], window[:, BLOCK:]
        wide = jnp.concatenate(
            [real, jnp.where(lane == 0, 0.0, imag), jnp.where(lane == 0, -imag, real)], axis=1
        )
        w = mm(gather_twice, jnp.concatenate(halves(wide), axis=0))
        y = mm3(inbox[:, pl.ds(pl.multiple_of(j * BLOCK, BLOCK), BLOCK)], fwd_high, fwd_low)
        y_real, y_imag = y[:, :BLOCK], y[:, BLOCK:]
        w_real, w_imag, w_other = w[:, :BLOCK], w[:, BLOCK : 2 * BLOCK], w[:, 2 * BLOCK :]
        corr[:, :BLOCK] += y_real * w_real + y_imag * w_imag
        corr[:, BLOCK:] += y_real * w_imag - y_imag * w_other

    lagged = mm3(corr[...], inv_high_ref[...], inv_low_ref[...])
    lag_out[...] = lagged
    high, low = halves(lagged)
    rec_out[...] = mm(pick, high) + mm(pick, low)

    @pl.loop(1, n)
    def _(k):
        d = lax.rem(me + k, n)
        rec_copy(d, me).start()
        lag_copy(d, me).start()

    lag_in[mine, :] = lag_out[mine, :]
    mine_rec = pl.ds(pl.multiple_of(me * REC_DEV, 8), REC_DEV)
    rec_in[mine_rec, :] = rec_out[mine_rec, :]

    @pl.loop(1, n)
    def _(k):
        d = lax.rem(me + (n - k), n)
        rec_copy(d, d).wait_recv()
        lag_copy(d, d).wait_recv()

    high, low = halves(lag_in[...])
    source_ref[...] = mm(take, high) + mm(take, low)
    total = rec_in[0:REC_DEV, :]
    for d in range(1, n):
        total = total + rec_in[d * REC_DEV : (d + 1) * REC_DEV, :]
    received_ref[...] = total

    @pl.loop(1, n)
    def _(k):
        d = lax.rem(me + k, n)
        label_copy(d, me).wait_send()
        trace_copy(d, me).wait_send()
        rec_copy(d, me).wait_send()
        lag_copy(d, me).wait_send()


def local(n, n_cmp, traces, statics, cmp_owner, cmp_offset, shot_id, receiver_id):
    count, samples = traces.shape
    cap = max(8, 2 * count // n)
    rows = n * cap

    def row(a):
        return a.reshape(1, count)

    tables = [jnp.asarray(t) for t in transform_tables(samples)]
    vmem = pl.BlockSpec(memory_space=pltpu.VMEM)
    return pl.pallas_call(
        functools.partial(kernel, n, n_cmp, cap),
        out_shape=(
            jax.ShapeDtypeStruct((SHOT_DEV, LAGS), f32),
            jax.ShapeDtypeStruct((REC_DEV, LAGS), f32),
        ),
        in_specs=[vmem] * 10,
        out_specs=(vmem, vmem),
        scratch_shapes=[
            pltpu.VMEM((2 * count, samples), bf16),
            pltpu.VMEM((rows, samples), f32),
            pltpu.VMEM((rows, samples), f32),
            pltpu.VMEM((n, BLOCK), f32),
            pltpu.VMEM((n, 1, BLOCK), f32),
            pltpu.VMEM((n, 1, BLOCK), f32),
            pltpu.VMEM((samples // BLOCK + 1, CMP_DEV, 2 * BLOCK), f32),
            pltpu.VMEM((rows, 2 * BLOCK), f32),
            pltpu.VMEM((rows, LAGS), f32),
            pltpu.VMEM((rows, LAGS), f32),
            pltpu.VMEM((n * REC_DEV, LAGS), f32),
            pltpu.VMEM((n * REC_DEV, LAGS), f32),
            pltpu.SemaphoreType.DMA((4, n)),
            pltpu.SemaphoreType.DMA((4, n)),
        ],
        compiler_params=pltpu.CompilerParams(
            collective_id=0, has_side_effects=True, vmem_limit_bytes=48 * 1024 * 1024
        ),
    )(row(cmp_owner), row(cmp_offset), row(shot_id), row(receiver_id), row(statics), traces, *tables)


def solution(mesh):
    axes = ("shot", "cmp")
    n = mesh.shape["shot"] * mesh.shape["cmp"]
    return jax.shard_map(
        functools.partial(local, n, mesh.shape["cmp"]),
        mesh=mesh,
        in_specs=(P(axes, None), P(axes), P(axes, None), P(axes), P(axes), P(axes)),
        out_specs=(P(axes, None), P(axes, None)),
        check_vma=False,
    )
```

```python
import functools

import jax
import jax.numpy as jnp
import ml_dtypes
import numpy as np
from jax import lax
from jax.experimental import pallas as pl
from jax.experimental.pallas import tpu as pltpu
from jax.sharding import PartitionSpec as P

LAGS = 128
MAX_SHIFT = 24
CMP_DEV = 32
SHOT_DEV = 16
REC_DEV = 16
BLOCK = 128
PARTS = 3
STACK_SCALE = 0.125

f32 = jnp.float32
bf16 = jnp.bfloat16
MESH = pl.DeviceIdType.MESH


def transform_tables(sample_total):
    u = np.arange(BLOCK)[:, None]
    f = np.arange(BLOCK)[None, :]
    angle = 2 * np.pi * ((u * f) % 256) / 256
    imag = -np.sin(angle)
    imag[:, 0] = 1 - 2 * (np.arange(BLOCK) % 2)
    forward = np.concatenate([np.cos(angle), imag], axis=1)
    weight = np.full((BLOCK, 1), 2.0)
    weight[0] = 1
    back_imag = -2 * np.sin(angle)
    back_imag[0] = 1 - 2 * (np.arange(BLOCK) % 2)
    inverse = np.concatenate([weight * np.cos(angle), back_imag], axis=0)
    inverse = inverse / 256 / sample_total * STACK_SCALE
    tables = []
    for table in (forward, inverse):
        high = table.astype(ml_dtypes.bfloat16)
        low = (table - high.astype(np.float64)).astype(ml_dtypes.bfloat16)
        tables += [high, low]
    return tables


def halves(x):
    high = x.astype(bf16)
    return high, (x - high.astype(f32)).astype(bf16)


def mm(a, b):
    return jnp.dot(a, b, preferred_element_type=f32)


def mm_nt(a, b):
    return lax.dot_general(a, b, (((1,), (1,)), ((), ())), preferred_element_type=f32)


def mm3(a, b_high, b_low):
    high, low = halves(a)
    return mm(high, b_high) + mm(low, b_high) + mm(high, b_low)


def iota(shape, dim):
    return lax.broadcasted_iota(jnp.int32, shape, dim)


def onehot(mask):
    return jnp.where(mask, 1.0, 0.0).astype(bf16)


def exact_dot(a, b):
    return jnp.dot(a, b, precision=lax.Precision.HIGHEST, preferred_element_type=f32)


def kernel(
    n, n_cmp, cap,
    owner_any, offset_any, shot_any, receiver_any, statics_any, traces_any,
    fwd_high_any, fwd_low_any, inv_high_any, inv_low_any,
    source_ref, received_ref,
    owner_ref, offset_ref, shot_ref, receiver_ref, statics_ref, traces_ref,
    fwd_high_ref, fwd_low_ref, inv_high_ref, inv_low_ref,
    shifted, outbox, inbox, label_rows, label_out, label_in, spectra, corr, lag_out, lag_in, rec_out, rec_in,
    send_sem, recv_sem, load_sem,
):
    rows = n * cap
    traces, samples = traces_ref.shape
    blocks = samples // BLOCK
    part = samples // PARTS
    per_part = blocks // PARTS
    me = lax.axis_index("shot") * n_cmp + lax.axis_index("cmp")

    def place(d):
        return (d // n_cmp, lax.rem(d, n_cmp))

    loads = [
        pltpu.make_async_copy(here, there, load_sem.at[i])
        for i, (here, there) in enumerate(
            (
                (owner_any, owner_ref),
                (offset_any, offset_ref),
                (shot_any, shot_ref),
                (receiver_any, receiver_ref),
                (statics_any, statics_ref),
                (traces_any, traces_ref),
                (fwd_high_any, fwd_high_ref),
                (fwd_low_any, fwd_low_ref),
                (inv_high_any, inv_high_ref),
                (inv_low_any, inv_low_ref),
            )
        )
    ]
    for load in loads:
        load.start()

    barrier = pltpu.get_barrier_semaphore()

    @pl.loop(1, n)
    def _(k):
        pl.semaphore_signal(barrier, inc=1, device_id=place(lax.rem(me + k, n)), device_id_type=MESH)

    def trace_copy(c, d, slot):
        columns = pl.ds(c * part, part)
        return pltpu.make_async_remote_copy(
            src_ref=outbox.at[pl.ds(pl.multiple_of(d * cap, 8), cap), columns],
            dst_ref=inbox.at[pl.ds(pl.multiple_of(slot * cap, 8), cap), columns],
            send_sem=send_sem.at[c, d], recv_sem=recv_sem.at[c, slot], device_id=place(d), device_id_type=MESH,
        )

    def label_copy(d, slot):
        return pltpu.make_async_remote_copy(
            src_ref=label_out.at[d], dst_ref=label_in.at[slot],
            send_sem=send_sem.at[PARTS, d], recv_sem=recv_sem.at[PARTS, slot], device_id=place(d), device_id_type=MESH,
        )

    def lag_copy(d, slot):
        return pltpu.make_async_remote_copy(
            src_ref=lag_out.at[pl.ds(pl.multiple_of(d * cap, 8), cap)],
            dst_ref=lag_in.at[pl.ds(pl.multiple_of(slot * cap, 8), cap)],
            send_sem=send_sem.at[PARTS + 1, d], recv_sem=recv_sem.at[PARTS + 1, slot], device_id=place(d), device_id_type=MESH,
        )

    def rec_copy(d, slot):
        return pltpu.make_async_remote_copy(
            src_ref=rec_out.at[pl.ds(pl.multiple_of(d * REC_DEV, 8), REC_DEV)],
            dst_ref=rec_in.at[pl.ds(pl.multiple_of(slot * REC_DEV, 8), REC_DEV)],
            send_sem=send_sem.at[PARTS + 2, d], recv_sem=recv_sem.at[PARTS + 2, slot], device_id=place(d), device_id_type=MESH,
        )

    for load in loads[:5]:
        load.wait()

    owner = owner_ref[...]
    member = iota((n, traces), 0) == owner
    upper = onehot(iota((traces, traces), 0) <= iota((traces, traces), 1))
    counts = mm(onehot(member), upper)
    rank = jnp.sum(jnp.where(member, counts, 0.0), axis=0, keepdims=True).astype(jnp.int32) - 1
    target = owner * cap + rank
    put = onehot(iota((rows, traces), 0) == target)
    put_twice = jnp.concatenate([put, put], axis=1)

    seat = iota((BLOCK, traces), 0)
    bins_here = jnp.where(member, (offset_ref[...] + 1).astype(f32), 0.0)
    rec_here = jnp.where(member, (receiver_ref[...] + 1).astype(f32), 0.0)

    def exact_nt(a, b):
        return lax.dot_general(
            a, b, (((1,), (1,)), ((), ())), precision=lax.Precision.HIGHEST, preferred_element_type=f32
        )

    label_rows[...] = exact_nt(bins_here, jnp.where(seat == rank, 1.0, 0.0)) + exact_nt(
        rec_here, jnp.where(seat == rank + 64, 1.0, 0.0)
    )

    @pl.loop(0, n)
    def _(d):
        label_out[d] = label_rows[pl.ds(d, 1), :]

    pl.semaphore_wait(barrier, n - 1)

    @pl.loop(1, n)
    def _(k):
        d = lax.rem(me + k, n)
        label_copy(d, me).start()

    label_in[me] = label_out[me]
    mine = pl.ds(pl.multiple_of(me * cap, 8), cap)

    eye = iota((traces, traces), 0) == iota((traces, traces), 1)
    amount = jnp.sum(jnp.where(eye, statics_ref[...], 0), axis=1, keepdims=True) + MAX_SHIFT
    step = 16
    width = part + 2 * BLOCK
    loads[5].wait()
    for c in range(PARTS):
        low_end, high_end = c * part - BLOCK, (c + 1) * part + BLOCK
        columns = slice(c * part, (c + 1) * part)
        for first in range(0, traces, step):
            row = traces_ref[first : first + step, max(low_end, 0) : min(high_end, samples)]
            edge = jnp.zeros((step, BLOCK), f32)
            if low_end < 0:
                row = jnp.concatenate([edge, row], axis=1)
            if high_end > samples:
                row = jnp.concatenate([row, edge], axis=1)
            here = amount[first : first + step]
            row = pltpu.roll(row, width - MAX_SHIFT, 1)
            for bit in range((2 * MAX_SHIFT).bit_length()):
                row = jnp.where((here >> bit) & 1 == 1, pltpu.roll(row, 1 << bit, 1), row)
            high, low = halves(row[:, BLOCK : BLOCK + part])
            shifted[first : first + step, columns] = high
            shifted[traces + first : traces + first + step, columns] = low
        outbox[:, columns] = mm(put_twice, shifted[:, columns])

        @pl.loop(1, n)
        def _(k):
            d = lax.rem(me + k, n)
            trace_copy(c, d, me).start()

        inbox[mine, columns] = outbox[mine, columns]

    own_shot = onehot(iota((SHOT_DEV, traces), 0) == lax.rem(shot_ref[...], SHOT_DEV))
    take = mm_nt(own_shot, put).astype(bf16)

    @pl.loop(1, n)
    def _(k):
        d = lax.rem(me + (n - k), n)
        label_copy(d, d).wait_recv()

    @pl.loop(0, n)
    def _(d):
        label_rows[pl.ds(d, 1), :] = label_in[d]

    labels = label_rows[...]
    spread = jnp.where(iota((rows, n), 0) // cap == iota((rows, n), 1), 1.0, 0.0)
    slot_col = iota((rows, BLOCK), 0) % cap
    lane_col = iota((rows, BLOCK), 1)
    per_slot = exact_dot(spread, labels)
    bin_col = jnp.sum(jnp.where(slot_col == lane_col, per_slot, 0.0), axis=1, keepdims=True).astype(jnp.int32) - 1
    slot_row = iota((BLOCK, rows), 1) % cap
    lane_row = iota((BLOCK, rows), 0)
    mine_row = iota((n, rows), 1) // cap == iota((n, rows), 0)
    bin_all = exact_dot(labels, jnp.where(slot_row == lane_row, 1.0, 0.0))
    rec_all = exact_dot(labels, jnp.where(slot_row + 64 == lane_row, 1.0, 0.0))
    bin_row = jnp.sum(jnp.where(mine_row, bin_all, 0.0), axis=0, keepdims=True).astype(jnp.int32) - 1
    rec_row = jnp.sum(jnp.where(mine_row, rec_all, 0.0), axis=0, keepdims=True).astype(jnp.int32) - 1
    gather = onehot(iota((rows, CMP_DEV), 1) == bin_col)
    gather_twice = jnp.concatenate([gather, gather], axis=1)
    stack = onehot(iota((CMP_DEV, rows), 0) == bin_row)
    pick = onehot(iota((REC_DEV * n, rows), 0) == rec_row)

    for load in loads[6:]:
        load.wait()
    fwd_high, fwd_low = fwd_high_ref[...], fwd_low_ref[...]
    lane = iota((CMP_DEV, BLOCK), 1)
    turn = (1 - 2 * (iota((CMP_DEV, 2 * BLOCK), 1) % 2)).astype(f32)
    corr[...] = jnp.zeros_like(corr)
    half = LAGS // 2
    before = jnp.zeros((CMP_DEV, half), f32)

    def block_spectrum(pilot, before):
        return mm3(jnp.concatenate([before, pilot[:, :half]], axis=1), fwd_high, fwd_low)

    def add_block(j):
        window = spectra[j] + turn * spectra[j + 1]
        real, imag = window[:, :BLOCK], window[:, BLOCK:]
        wide = jnp.concatenate(
            [real, jnp.where(lane == 0, 0.0, imag), jnp.where(lane == 0, -imag, real)], axis=1
        )
        w = mm(gather_twice, jnp.concatenate(halves(wide), axis=0))
        y = mm3(inbox[:, pl.ds(j * BLOCK, BLOCK)], fwd_high, fwd_low)
        y_real, y_imag = y[:, :BLOCK], y[:, BLOCK:]
        w_real, w_imag, w_other = w[:, :BLOCK], w[:, BLOCK : 2 * BLOCK], w[:, 2 * BLOCK :]
        corr[:, :BLOCK] += y_real * w_real + y_imag * w_imag
        corr[:, BLOCK:] += y_real * w_imag - y_imag * w_other

    for c in range(PARTS):

        @pl.loop(1, n)
        def _(k):
            d = lax.rem(me + (n - k), n)
            trace_copy(c, d, d).wait_recv()

        for j in range(c * per_part, (c + 1) * per_part):
            high, low = halves(inbox[:, j * BLOCK : (j + 1) * BLOCK])
            pilot = mm(stack, high) + mm(stack, low)
            spectra[j] = block_spectrum(pilot, before)
            before = pilot[:, half:]
            if j > 0:
                add_block(j - 1)
    spectra[blocks] = block_spectrum(jnp.zeros((CMP_DEV, BLOCK), f32), before)
    add_block(blocks - 1)

    lagged = mm3(corr[...], inv_high_ref[...], inv_low_ref[...])
    lag_out[...] = lagged

    @pl.loop(1, n)
    def _(k):
        d = lax.rem(me + k, n)
        lag_copy(d, me).start()

    high, low = halves(lagged)
    rec_out[...] = mm(pick, high) + mm(pick, low)

    @pl.loop(1, n)
    def _(k):
        d = lax.rem(me + k, n)
        rec_copy(d, me).start()

    lag_in[mine, :] = lag_out[mine, :]
    mine_rec = pl.ds(pl.multiple_of(me * REC_DEV, 8), REC_DEV)
    rec_in[mine_rec, :] = rec_out[mine_rec, :]

    @pl.loop(1, n)
    def _(k):
        d = lax.rem(me + (n - k), n)
        rec_copy(d, d).wait_recv()
        lag_copy(d, d).wait_recv()

    high, low = halves(lag_in[...])
    source_ref[...] = mm(take, high) + mm(take, low)
    total = rec_in[0:REC_DEV, :]
    for d in range(1, n):
        total = total + rec_in[d * REC_DEV : (d + 1) * REC_DEV, :]
    received_ref[...] = total

    @pl.loop(1, n)
    def _(k):
        d = lax.rem(me + k, n)
        label_copy(d, me).wait_send()
        for c in range(PARTS):
            trace_copy(c, d, me).wait_send()
        rec_copy(d, me).wait_send()
        lag_copy(d, me).wait_send()


def local(n, n_cmp, traces, statics, cmp_owner, cmp_offset, shot_id, receiver_id):
    count, samples = traces.shape
    cap = max(8, 2 * count // n)
    rows = n * cap

    def row(a):
        return a.reshape(1, count)

    tables = [jnp.asarray(t) for t in transform_tables(samples)]
    vmem = pl.BlockSpec(memory_space=pltpu.VMEM)
    return pl.pallas_call(
        functools.partial(kernel, n, n_cmp, cap),
        out_shape=(
            jax.ShapeDtypeStruct((SHOT_DEV, LAGS), f32),
            jax.ShapeDtypeStruct((REC_DEV, LAGS), f32),
        ),
        in_specs=[pl.BlockSpec(memory_space=pl.ANY)] * 10,
        out_specs=(vmem, vmem),
        scratch_shapes=[pltpu.VMEM((1, count), jnp.int32) for _ in range(5)]
        + [pltpu.VMEM((count, samples), f32)]
        + [pltpu.VMEM(t.shape, bf16) for t in tables]
        + [
            pltpu.VMEM((2 * count, samples), bf16),
            pltpu.VMEM((rows, samples), f32),
            pltpu.VMEM((rows, samples), f32),
            pltpu.VMEM((n, BLOCK), f32),
            pltpu.VMEM((n, 1, BLOCK), f32),
            pltpu.VMEM((n, 1, BLOCK), f32),
            pltpu.VMEM((samples // BLOCK + 1, CMP_DEV, 2 * BLOCK), f32),
            pltpu.VMEM((rows, 2 * BLOCK), f32),
            pltpu.VMEM((rows, LAGS), f32),
            pltpu.VMEM((rows, LAGS), f32),
            pltpu.VMEM((n * REC_DEV, LAGS), f32),
            pltpu.VMEM((n * REC_DEV, LAGS), f32),
            pltpu.SemaphoreType.DMA((PARTS + 3, n)),
            pltpu.SemaphoreType.DMA((PARTS + 3, n)),
            pltpu.SemaphoreType.DMA((10,)),
        ],
        compiler_params=pltpu.CompilerParams(
            collective_id=0, has_side_effects=True, vmem_limit_bytes=48 * 1024 * 1024
        ),
    )(row(cmp_owner), row(cmp_offset), row(shot_id), row(receiver_id), row(statics), traces, *tables)


def solution(mesh):
    axes = ("shot", "cmp")
    n = mesh.shape["shot"] * mesh.shape["cmp"]
    return jax.shard_map(
        functools.partial(local, n, mesh.shape["cmp"]),
        mesh=mesh,
        in_specs=(P(axes, None), P(axes), P(axes, None), P(axes), P(axes), P(axes)),
        out_specs=(P(axes, None), P(axes, None)),
        check_vma=False,
    )
```

```python
import functools

import jax
import jax.numpy as jnp
import ml_dtypes
import numpy as np
from jax import lax
from jax.experimental import pallas as pl
from jax.experimental.pallas import tpu as pltpu
from jax.sharding import PartitionSpec as P

LAGS = 128
MAX_SHIFT = 24
CMP_DEV = 32
SHOT_DEV = 16
REC_DEV = 16
BLOCK = 128
PARTS = 3
STACK_SCALE = 0.125

f32 = jnp.float32
bf16 = jnp.bfloat16
MESH = pl.DeviceIdType.MESH


def transform_tables(sample_total):
    u = np.arange(BLOCK)[:, None]
    f = np.arange(BLOCK)[None, :]
    angle = 2 * np.pi * ((u * f) % 256) / 256
    imag = -np.sin(angle)
    imag[:, 0] = 1 - 2 * (np.arange(BLOCK) % 2)
    forward = np.concatenate([np.cos(angle), imag], axis=1)
    weight = np.full((BLOCK, 1), 2.0)
    weight[0] = 1
    back_imag = -2 * np.sin(angle)
    back_imag[0] = 1 - 2 * (np.arange(BLOCK) % 2)
    inverse = np.concatenate([weight * np.cos(angle), back_imag], axis=0)
    inverse = inverse / 256 / sample_total * STACK_SCALE
    tables = []
    for table in (forward, inverse):
        high = table.astype(ml_dtypes.bfloat16)
        low = (table - high.astype(np.float64)).astype(ml_dtypes.bfloat16)
        tables += [high, low]
    return tables


def halves(x):
    high = x.astype(bf16)
    return high, (x - high.astype(f32)).astype(bf16)


def mm(a, b):
    return jnp.dot(a, b, preferred_element_type=f32)


def mm_nt(a, b):
    return lax.dot_general(a, b, (((1,), (1,)), ((), ())), preferred_element_type=f32)


def mm3(a, b_high, b_low):
    high, low = halves(a)
    return mm(high, b_high) + mm(low, b_high) + mm(high, b_low)


def iota(shape, dim):
    return lax.broadcasted_iota(jnp.int32, shape, dim)


def onehot(mask):
    return jnp.where(mask, 1.0, 0.0).astype(bf16)


def exact_dot(a, b):
    return jnp.dot(a, b, precision=lax.Precision.HIGHEST, preferred_element_type=f32)


def kernel(
    n, n_cmp, cap,
    owner_any, offset_any, shot_any, receiver_any, statics_any, traces_any,
    fwd_high_any, fwd_low_any, inv_high_any, inv_low_any,
    source_ref, received_ref,
    owner_ref, offset_ref, shot_ref, receiver_ref, statics_ref, traces_ref,
    fwd_high_ref, fwd_low_ref, inv_high_ref, inv_low_ref,
    shifted, outbox, inbox, label_rows, label_out, label_in, spectra, corr, lag_out, lag_in, rec_out, rec_side, rec_in,
    send_sem, recv_sem, side_sem, load_sem,
):
    rows = n * cap
    traces, samples = traces_ref.shape
    blocks = samples // BLOCK
    part = samples // PARTS
    per_part = blocks // PARTS
    shot, cmp = lax.axis_index("shot"), lax.axis_index("cmp")
    me = shot * n_cmp + cmp
    pairs = n // n_cmp // 2
    core = lax.rem(shot, 2)
    team = n // 2
    rank_in_team = shot // 2 * n_cmp + cmp
    shot_rows = n_cmp * REC_DEV

    def place(d):
        return (d // n_cmp, lax.rem(d, n_cmp))

    loads = [
        pltpu.make_async_copy(here, there, load_sem.at[i])
        for i, (here, there) in enumerate(
            (
                (owner_any, owner_ref),
                (offset_any, offset_ref),
                (shot_any, shot_ref),
                (receiver_any, receiver_ref),
                (statics_any, statics_ref),
                (traces_any, traces_ref),
                (fwd_high_any, fwd_high_ref),
                (fwd_low_any, fwd_low_ref),
                (inv_high_any, inv_high_ref),
                (inv_low_any, inv_low_ref),
            )
        )
    ]
    for load in loads:
        load.start()

    barrier = pltpu.get_barrier_semaphore()

    @pl.loop(1, n)
    def _(k):
        pl.semaphore_signal(barrier, inc=1, device_id=place(lax.rem(me + k, n)), device_id_type=MESH)

    def trace_copy(c, d, slot):
        columns = pl.ds(c * part, part)
        return pltpu.make_async_remote_copy(
            src_ref=outbox.at[pl.ds(pl.multiple_of(d * cap, 8), cap), columns],
            dst_ref=inbox.at[pl.ds(pl.multiple_of(slot * cap, 8), cap), columns],
            send_sem=send_sem.at[c, d], recv_sem=recv_sem.at[c, slot], device_id=place(d), device_id_type=MESH,
        )

    def label_copy(d, slot):
        return pltpu.make_async_remote_copy(
            src_ref=label_out.at[d], dst_ref=label_in.at[slot],
            send_sem=send_sem.at[PARTS, d], recv_sem=recv_sem.at[PARTS, slot], device_id=place(d), device_id_type=MESH,
        )

    def lag_copy(d, slot):
        return pltpu.make_async_remote_copy(
            src_ref=lag_out.at[pl.ds(pl.multiple_of(d * cap, 8), cap)],
            dst_ref=lag_in.at[pl.ds(pl.multiple_of(slot * cap, 8), cap)],
            send_sem=send_sem.at[PARTS + 1, d], recv_sem=recv_sem.at[PARTS + 1, slot], device_id=place(d), device_id_type=MESH,
        )

    def shot_block(i, c):
        return pl.ds(pl.multiple_of((2 * i + c) * shot_rows, 8), shot_rows)

    def side_copy(i):
        return pltpu.make_async_remote_copy(
            src_ref=rec_out.at[shot_block(i, 1 - core)],
            dst_ref=rec_side.at[pl.ds(i * shot_rows, shot_rows)],
            send_sem=side_sem.at[0, i], recv_sem=side_sem.at[1, i],
            device_id=(shot + 1 - 2 * core, cmp), device_id_type=MESH,
        )

    def rec_copy(p, slot):
        d = (2 * (p // n_cmp) + core) * n_cmp + lax.rem(p, n_cmp)
        return pltpu.make_async_remote_copy(
            src_ref=rec_out.at[pl.ds(pl.multiple_of(d * REC_DEV, 8), REC_DEV)],
            dst_ref=rec_in.at[pl.ds(pl.multiple_of(slot * REC_DEV, 8), REC_DEV)],
            send_sem=send_sem.at[PARTS + 2, p], recv_sem=recv_sem.at[PARTS + 2, slot],
            device_id=place(d), device_id_type=MESH,
        )

    for load in loads[:5]:
        load.wait()

    owner = owner_ref[...]
    member = iota((n, traces), 0) == owner
    upper = onehot(iota((traces, traces), 0) <= iota((traces, traces), 1))
    counts = mm(onehot(member), upper)
    rank = jnp.sum(jnp.where(member, counts, 0.0), axis=0, keepdims=True).astype(jnp.int32) - 1
    target = owner * cap + rank
    put = onehot(iota((rows, traces), 0) == target)
    put_twice = jnp.concatenate([put, put], axis=1)

    seat = iota((BLOCK, traces), 0)
    bins_here = jnp.where(member, (offset_ref[...] + 1).astype(f32), 0.0)
    rec_here = jnp.where(member, (receiver_ref[...] + 1).astype(f32), 0.0)

    def exact_nt(a, b):
        return lax.dot_general(
            a, b, (((1,), (1,)), ((), ())), precision=lax.Precision.HIGHEST, preferred_element_type=f32
        )

    label_rows[...] = exact_nt(bins_here, jnp.where(seat == rank, 1.0, 0.0)) + exact_nt(
        rec_here, jnp.where(seat == rank + 64, 1.0, 0.0)
    )

    @pl.loop(0, n)
    def _(d):
        label_out[d] = label_rows[pl.ds(d, 1), :]

    pl.semaphore_wait(barrier, n - 1)

    @pl.loop(1, n)
    def _(k):
        d = lax.rem(me + k, n)
        label_copy(d, me).start()

    label_in[me] = label_out[me]
    mine = pl.ds(pl.multiple_of(me * cap, 8), cap)

    eye = iota((traces, traces), 0) == iota((traces, traces), 1)
    amount = jnp.sum(jnp.where(eye, statics_ref[...], 0), axis=1, keepdims=True) + MAX_SHIFT
    step = 16
    width = part + 2 * BLOCK
    loads[5].wait()
    for c in range(PARTS):
        low_end, high_end = c * part - BLOCK, (c + 1) * part + BLOCK
        columns = slice(c * part, (c + 1) * part)
        for first in range(0, traces, step):
            row = traces_ref[first : first + step, max(low_end, 0) : min(high_end, samples)]
            edge = jnp.zeros((step, BLOCK), f32)
            if low_end < 0:
                row = jnp.concatenate([edge, row], axis=1)
            if high_end > samples:
                row = jnp.concatenate([row, edge], axis=1)
            here = amount[first : first + step]
            row = pltpu.roll(row, width - MAX_SHIFT, 1)
            for bit in range((2 * MAX_SHIFT).bit_length()):
                row = jnp.where((here >> bit) & 1 == 1, pltpu.roll(row, 1 << bit, 1), row)
            high, low = halves(row[:, BLOCK : BLOCK + part])
            shifted[first : first + step, columns] = high
            shifted[traces + first : traces + first + step, columns] = low
        outbox[:, columns] = mm(put_twice, shifted[:, columns])

        @pl.loop(1, n)
        def _(k):
            d = lax.rem(me + k, n)
            trace_copy(c, d, me).start()

        inbox[mine, columns] = outbox[mine, columns]

    own_shot = onehot(iota((SHOT_DEV, traces), 0) == lax.rem(shot_ref[...], SHOT_DEV))
    take = mm_nt(own_shot, put).astype(bf16)

    @pl.loop(1, n)
    def _(k):
        d = lax.rem(me + (n - k), n)
        label_copy(d, d).wait_recv()

    @pl.loop(0, n)
    def _(d):
        label_rows[pl.ds(d, 1), :] = label_in[d]

    labels = label_rows[...]
    spread = jnp.where(iota((rows, n), 0) // cap == iota((rows, n), 1), 1.0, 0.0)
    slot_col = iota((rows, BLOCK), 0) % cap
    lane_col = iota((rows, BLOCK), 1)
    per_slot = exact_dot(spread, labels)
    bin_col = jnp.sum(jnp.where(slot_col == lane_col, per_slot, 0.0), axis=1, keepdims=True).astype(jnp.int32) - 1
    slot_row = iota((BLOCK, rows), 1) % cap
    lane_row = iota((BLOCK, rows), 0)
    mine_row = iota((n, rows), 1) // cap == iota((n, rows), 0)
    bin_all = exact_dot(labels, jnp.where(slot_row == lane_row, 1.0, 0.0))
    rec_all = exact_dot(labels, jnp.where(slot_row + 64 == lane_row, 1.0, 0.0))
    bin_row = jnp.sum(jnp.where(mine_row, bin_all, 0.0), axis=0, keepdims=True).astype(jnp.int32) - 1
    rec_row = jnp.sum(jnp.where(mine_row, rec_all, 0.0), axis=0, keepdims=True).astype(jnp.int32) - 1
    gather = onehot(iota((rows, CMP_DEV), 1) == bin_col)
    gather_twice = jnp.concatenate([gather, gather], axis=1)
    stack = onehot(iota((CMP_DEV, rows), 0) == bin_row)
    pick = onehot(iota((REC_DEV * n, rows), 0) == rec_row)

    for load in loads[6:]:
        load.wait()
    fwd_high, fwd_low = fwd_high_ref[...], fwd_low_ref[...]
    lane = iota((CMP_DEV, BLOCK), 1)
    turn = (1 - 2 * (iota((CMP_DEV, 2 * BLOCK), 1) % 2)).astype(f32)
    corr[...] = jnp.zeros_like(corr)
    half = LAGS // 2
    before = jnp.zeros((CMP_DEV, half), f32)

    def block_spectrum(pilot, before):
        return mm3(jnp.concatenate([before, pilot[:, :half]], axis=1), fwd_high, fwd_low)

    def add_block(j):
        window = spectra[j] + turn * spectra[j + 1]
        real, imag = window[:, :BLOCK], window[:, BLOCK:]
        wide = jnp.concatenate(
            [real, jnp.where(lane == 0, 0.0, imag), jnp.where(lane == 0, -imag, real)], axis=1
        )
        w = mm(gather_twice, jnp.concatenate(halves(wide), axis=0))
        y = mm3(inbox[:, pl.ds(j * BLOCK, BLOCK)], fwd_high, fwd_low)
        y_real, y_imag = y[:, :BLOCK], y[:, BLOCK:]
        w_real, w_imag, w_other = w[:, :BLOCK], w[:, BLOCK : 2 * BLOCK], w[:, 2 * BLOCK :]
        corr[:, :BLOCK] += y_real * w_real + y_imag * w_imag
        corr[:, BLOCK:] += y_real * w_imag - y_imag * w_other

    for c in range(PARTS):

        @pl.loop(1, n)
        def _(k):
            d = lax.rem(me + (n - k), n)
            trace_copy(c, d, d).wait_recv()

        for j in range(c * per_part, (c + 1) * per_part):
            high, low = halves(inbox[:, j * BLOCK : (j + 1) * BLOCK])
            pilot = mm(stack, high) + mm(stack, low)
            spectra[j] = block_spectrum(pilot, before)
            before = pilot[:, half:]
            if j > 0:
                add_block(j - 1)
    spectra[blocks] = block_spectrum(jnp.zeros((CMP_DEV, BLOCK), f32), before)
    add_block(blocks - 1)

    lagged = mm3(corr[...], inv_high_ref[...], inv_low_ref[...])
    lag_out[...] = lagged

    @pl.loop(1, n)
    def _(k):
        d = lax.rem(me + k, n)
        lag_copy(d, me).start()

    high, low = halves(lagged)
    rec_out[...] = mm(pick, high) + mm(pick, low)

    for i in range(pairs):
        side_copy(i).start()

    lag_in[mine, :] = lag_out[mine, :]
    for i in range(pairs):
        side_copy(i).wait_recv()
        rec_out[shot_block(i, core), :] += rec_side[i * shot_rows : (i + 1) * shot_rows, :]

    @pl.loop(1, team)
    def _(k):
        rec_copy(lax.rem(rank_in_team + k, team), rank_in_team).start()

    own_rows = pl.ds(pl.multiple_of(rank_in_team * REC_DEV, 8), REC_DEV)
    rec_in[own_rows, :] = rec_out[pl.ds(pl.multiple_of(me * REC_DEV, 8), REC_DEV), :]

    @pl.loop(1, n)
    def _(k):
        d = lax.rem(me + (n - k), n)
        lag_copy(d, d).wait_recv()

    high, low = halves(lag_in[...])
    source_ref[...] = mm(take, high) + mm(take, low)

    @pl.loop(1, team)
    def _(k):
        p = lax.rem(rank_in_team + (team - k), team)
        rec_copy(p, p).wait_recv()

    total = rec_in[0:REC_DEV, :]
    for d in range(1, team):
        total = total + rec_in[d * REC_DEV : (d + 1) * REC_DEV, :]
    received_ref[...] = total

    @pl.loop(1, n)
    def _(k):
        d = lax.rem(me + k, n)
        label_copy(d, me).wait_send()
        for c in range(PARTS):
            trace_copy(c, d, me).wait_send()
        lag_copy(d, me).wait_send()

    for i in range(pairs):
        side_copy(i).wait_send()

    @pl.loop(1, team)
    def _(k):
        rec_copy(lax.rem(rank_in_team + k, team), rank_in_team).wait_send()


def local(n, n_cmp, traces, statics, cmp_owner, cmp_offset, shot_id, receiver_id):
    count, samples = traces.shape
    cap = max(8, 2 * count // n)
    rows = n * cap

    def row(a):
        return a.reshape(1, count)

    tables = [jnp.asarray(t) for t in transform_tables(samples)]
    vmem = pl.BlockSpec(memory_space=pltpu.VMEM)
    return pl.pallas_call(
        functools.partial(kernel, n, n_cmp, cap),
        out_shape=(
            jax.ShapeDtypeStruct((SHOT_DEV, LAGS), f32),
            jax.ShapeDtypeStruct((REC_DEV, LAGS), f32),
        ),
        in_specs=[pl.BlockSpec(memory_space=pltpu.HBM)] * 10,
        out_specs=(vmem, vmem),
        scratch_shapes=[pltpu.VMEM((1, count), jnp.int32) for _ in range(5)]
        + [pltpu.VMEM((count, samples), f32)]
        + [pltpu.VMEM(t.shape, bf16) for t in tables]
        + [
            pltpu.VMEM((2 * count, samples), bf16),
            pltpu.VMEM((rows, samples), f32),
            pltpu.VMEM((rows, samples), f32),
            pltpu.VMEM((n, BLOCK), f32),
            pltpu.VMEM((n, 1, BLOCK), f32),
            pltpu.VMEM((n, 1, BLOCK), f32),
            pltpu.VMEM((samples // BLOCK + 1, CMP_DEV, 2 * BLOCK), f32),
            pltpu.VMEM((rows, 2 * BLOCK), f32),
            pltpu.VMEM((rows, LAGS), f32),
            pltpu.VMEM((rows, LAGS), f32),
            pltpu.VMEM((n * REC_DEV, LAGS), f32),
            pltpu.VMEM((n // 2 * REC_DEV, LAGS), f32),
            pltpu.VMEM((n // 2 * REC_DEV, LAGS), f32),
            pltpu.SemaphoreType.DMA((PARTS + 3, n)),
            pltpu.SemaphoreType.DMA((PARTS + 3, n)),
            pltpu.SemaphoreType.DMA((2, n // n_cmp // 2)),
            pltpu.SemaphoreType.DMA((10,)),
        ],
        compiler_params=pltpu.CompilerParams(
            collective_id=0, has_side_effects=True, vmem_limit_bytes=48 * 1024 * 1024
        ),
    )(row(cmp_owner), row(cmp_offset), row(shot_id), row(receiver_id), row(statics), traces, *tables)


def solution(mesh):
    axes = ("shot", "cmp")
    n = mesh.shape["shot"] * mesh.shape["cmp"]
    return jax.shard_map(
        functools.partial(local, n, mesh.shape["cmp"]),
        mesh=mesh,
        in_specs=(P(axes, None), P(axes), P(axes, None), P(axes), P(axes), P(axes)),
        out_specs=(P(axes, None), P(axes, None)),
        check_vma=False,
    )
```

```python
import functools

import jax
import jax.numpy as jnp
import ml_dtypes
import numpy as np
from jax import lax
from jax.experimental import pallas as pl
from jax.experimental.pallas import tpu as pltpu
from jax.sharding import PartitionSpec as P

LAGS = 128
MAX_SHIFT = 24
CMP_DEV = 32
SHOT_DEV = 16
REC_DEV = 16
BLOCK = 128
SIZES = (6, 6, 3)
PARTS = len(SIZES)
ENDS = tuple(sum(SIZES[:i]) for i in range(PARTS + 1))
STACK_SCALE = 0.125

f32 = jnp.float32
bf16 = jnp.bfloat16
MESH = pl.DeviceIdType.MESH


def transform_tables(sample_total):
    u = np.arange(BLOCK)[:, None]
    f = np.arange(BLOCK)[None, :]
    angle = 2 * np.pi * ((u * f) % 256) / 256
    imag = -np.sin(angle)
    imag[:, 0] = 1 - 2 * (np.arange(BLOCK) % 2)
    forward = np.concatenate([np.cos(angle), imag], axis=1)
    weight = np.full((BLOCK, 1), 2.0)
    weight[0] = 1
    back_imag = -2 * np.sin(angle)
    back_imag[0] = 1 - 2 * (np.arange(BLOCK) % 2)
    inverse = np.concatenate([weight * np.cos(angle), back_imag], axis=0)
    inverse = inverse / 256 / sample_total * STACK_SCALE
    tables = []
    for table in (forward, inverse):
        high = table.astype(ml_dtypes.bfloat16)
        low = (table - high.astype(np.float64)).astype(ml_dtypes.bfloat16)
        tables += [high, low]
    return tables


def halves(x):
    high = x.astype(bf16)
    return high, (x - high.astype(f32)).astype(bf16)


def mm(a, b):
    return jnp.dot(a, b, preferred_element_type=f32)


def mm_nt(a, b):
    return lax.dot_general(a, b, (((1,), (1,)), ((), ())), preferred_element_type=f32)


def mm3(a, b_high, b_low):
    high, low = halves(a)
    return mm(high, b_high) + mm(low, b_high) + mm(high, b_low)


def iota(shape, dim):
    return lax.broadcasted_iota(jnp.int32, shape, dim)


def onehot(mask):
    return jnp.where(mask, 1.0, 0.0).astype(bf16)


def exact_dot(a, b):
    return jnp.dot(a, b, precision=lax.Precision.HIGHEST, preferred_element_type=f32)


def kernel(
    n, n_cmp, cap,
    owner_any, offset_any, shot_any, receiver_any, statics_any, traces_any,
    fwd_high_any, fwd_low_any, inv_high_any, inv_low_any,
    source_ref, received_ref,
    owner_ref, offset_ref, shot_ref, receiver_ref, statics_ref, traces_ref,
    fwd_high_ref, fwd_low_ref, inv_high_ref, inv_low_ref,
    shifted, outbox, inbox, label_rows, label_out, label_in, spectra, corr, lag_out, lag_in, rec_out, rec_side, rec_in,
    send_sem, recv_sem, side_sem, load_sem,
):
    rows = n * cap
    traces, samples = traces_ref.shape
    blocks = samples // BLOCK
    shot, cmp = lax.axis_index("shot"), lax.axis_index("cmp")
    me = shot * n_cmp + cmp
    pairs = n // n_cmp // 2
    core = lax.rem(shot, 2)
    team = n // 2
    rank_in_team = shot // 2 * n_cmp + cmp
    shot_rows = n_cmp * REC_DEV

    def place(d):
        return (d // n_cmp, lax.rem(d, n_cmp))

    loads = [
        pltpu.make_async_copy(here, there, load_sem.at[i])
        for i, (here, there) in enumerate(
            (
                (owner_any, owner_ref),
                (offset_any, offset_ref),
                (shot_any, shot_ref),
                (receiver_any, receiver_ref),
                (statics_any, statics_ref),
                (traces_any, traces_ref),
                (fwd_high_any, fwd_high_ref),
                (fwd_low_any, fwd_low_ref),
                (inv_high_any, inv_high_ref),
                (inv_low_any, inv_low_ref),
            )
        )
    ]
    for load in loads:
        load.start()

    barrier = pltpu.get_barrier_semaphore()

    @pl.loop(1, n)
    def _(k):
        pl.semaphore_signal(barrier, inc=1, device_id=place(lax.rem(me + k, n)), device_id_type=MESH)

    def trace_copy(c, d, slot):
        columns = pl.ds(ENDS[c] * BLOCK, SIZES[c] * BLOCK)
        return pltpu.make_async_remote_copy(
            src_ref=outbox.at[pl.ds(pl.multiple_of(d * cap, 8), cap), columns],
            dst_ref=inbox.at[pl.ds(pl.multiple_of(slot * cap, 8), cap), columns],
            send_sem=send_sem.at[c, d], recv_sem=recv_sem.at[c, slot], device_id=place(d), device_id_type=MESH,
        )

    def label_copy(d, slot):
        return pltpu.make_async_remote_copy(
            src_ref=label_out.at[d], dst_ref=label_in.at[slot],
            send_sem=send_sem.at[PARTS, d], recv_sem=recv_sem.at[PARTS, slot], device_id=place(d), device_id_type=MESH,
        )

    def lag_copy(d, slot):
        return pltpu.make_async_remote_copy(
            src_ref=lag_out.at[pl.ds(pl.multiple_of(d * cap, 8), cap)],
            dst_ref=lag_in.at[pl.ds(pl.multiple_of(slot * cap, 8), cap)],
            send_sem=send_sem.at[PARTS + 1, d], recv_sem=recv_sem.at[PARTS + 1, slot], device_id=place(d), device_id_type=MESH,
        )

    def shot_block(i, c):
        return pl.ds(pl.multiple_of((2 * i + c) * shot_rows, 8), shot_rows)

    def side_copy(i):
        return pltpu.make_async_remote_copy(
            src_ref=rec_out.at[shot_block(i, 1 - core)],
            dst_ref=rec_side.at[pl.ds(i * shot_rows, shot_rows)],
            send_sem=side_sem.at[0, i], recv_sem=side_sem.at[1, i],
            device_id=(shot + 1 - 2 * core, cmp), device_id_type=MESH,
        )

    def rec_copy(p, slot):
        d = (2 * (p // n_cmp) + core) * n_cmp + lax.rem(p, n_cmp)
        return pltpu.make_async_remote_copy(
            src_ref=rec_out.at[pl.ds(pl.multiple_of(d * REC_DEV, 8), REC_DEV)],
            dst_ref=rec_in.at[pl.ds(pl.multiple_of(slot * REC_DEV, 8), REC_DEV)],
            send_sem=send_sem.at[PARTS + 2, p], recv_sem=recv_sem.at[PARTS + 2, slot],
            device_id=place(d), device_id_type=MESH,
        )

    for load in loads[:5]:
        load.wait()

    owner = owner_ref[...]
    member = iota((n, traces), 0) == owner
    upper = onehot(iota((traces, traces), 0) <= iota((traces, traces), 1))
    counts = mm(onehot(member), upper)
    rank = jnp.sum(jnp.where(member, counts, 0.0), axis=0, keepdims=True).astype(jnp.int32) - 1
    target = owner * cap + rank
    put = onehot(iota((rows, traces), 0) == target)
    put_twice = jnp.concatenate([put, put], axis=1)

    seat = iota((BLOCK, traces), 0)
    bins_here = jnp.where(member, (offset_ref[...] + 1).astype(f32), 0.0)
    rec_here = jnp.where(member, (receiver_ref[...] + 1).astype(f32), 0.0)

    def exact_nt(a, b):
        return lax.dot_general(
            a, b, (((1,), (1,)), ((), ())), precision=lax.Precision.HIGHEST, preferred_element_type=f32
        )

    label_rows[...] = exact_nt(bins_here, jnp.where(seat == rank, 1.0, 0.0)) + exact_nt(
        rec_here, jnp.where(seat == rank + 64, 1.0, 0.0)
    )

    @pl.loop(0, n)
    def _(d):
        label_out[d] = label_rows[pl.ds(d, 1), :]

    pl.semaphore_wait(barrier, n - 1)

    @pl.loop(1, n)
    def _(k):
        d = lax.rem(me + k, n)
        label_copy(d, me).start()

    label_in[me] = label_out[me]
    mine = pl.ds(pl.multiple_of(me * cap, 8), cap)

    eye = iota((traces, traces), 0) == iota((traces, traces), 1)
    amount = jnp.sum(jnp.where(eye, statics_ref[...], 0), axis=1, keepdims=True) + MAX_SHIFT
    step = 16
    loads[5].wait()
    for c in range(PARTS):
        part = SIZES[c] * BLOCK
        width = part + 2 * BLOCK
        low_end, high_end = (ENDS[c] - 1) * BLOCK, (ENDS[c + 1] + 1) * BLOCK
        columns = slice(ENDS[c] * BLOCK, ENDS[c + 1] * BLOCK)
        for first in range(0, traces, step):
            row = traces_ref[first : first + step, max(low_end, 0) : min(high_end, samples)]
            edge = jnp.zeros((step, BLOCK), f32)
            if low_end < 0:
                row = jnp.concatenate([edge, row], axis=1)
            if high_end > samples:
                row = jnp.concatenate([row, edge], axis=1)
            here = amount[first : first + step]
            row = pltpu.roll(row, width - MAX_SHIFT, 1)
            for bit in range((2 * MAX_SHIFT).bit_length()):
                row = jnp.where((here >> bit) & 1 == 1, pltpu.roll(row, 1 << bit, 1), row)
            high, low = halves(row[:, BLOCK : BLOCK + part])
            shifted[first : first + step, columns] = high
            shifted[traces + first : traces + first + step, columns] = low
        outbox[:, columns] = mm(put_twice, shifted[:, columns])

        @pl.loop(1, n)
        def _(k):
            d = lax.rem(me + k, n)
            trace_copy(c, d, me).start()

        inbox[mine, columns] = outbox[mine, columns]

    own_shot = onehot(iota((SHOT_DEV, traces), 0) == lax.rem(shot_ref[...], SHOT_DEV))
    take = mm_nt(own_shot, put).astype(bf16)

    @pl.loop(1, n)
    def _(k):
        d = lax.rem(me + (n - k), n)
        label_copy(d, d).wait_recv()

    @pl.loop(0, n)
    def _(d):
        label_rows[pl.ds(d, 1), :] = label_in[d]

    labels = label_rows[...]
    spread = jnp.where(iota((rows, n), 0) // cap == iota((rows, n), 1), 1.0, 0.0)
    slot_col = iota((rows, BLOCK), 0) % cap
    lane_col = iota((rows, BLOCK), 1)
    per_slot = exact_dot(spread, labels)
    bin_col = jnp.sum(jnp.where(slot_col == lane_col, per_slot, 0.0), axis=1, keepdims=True).astype(jnp.int32) - 1
    slot_row = iota((BLOCK, rows), 1) % cap
    lane_row = iota((BLOCK, rows), 0)
    mine_row = iota((n, rows), 1) // cap == iota((n, rows), 0)
    bin_all = exact_dot(labels, jnp.where(slot_row == lane_row, 1.0, 0.0))
    rec_all = exact_dot(labels, jnp.where(slot_row + 64 == lane_row, 1.0, 0.0))
    bin_row = jnp.sum(jnp.where(mine_row, bin_all, 0.0), axis=0, keepdims=True).astype(jnp.int32) - 1
    rec_row = jnp.sum(jnp.where(mine_row, rec_all, 0.0), axis=0, keepdims=True).astype(jnp.int32) - 1
    gather = onehot(iota((rows, CMP_DEV), 1) == bin_col)
    gather_twice = jnp.concatenate([gather, gather], axis=1)
    stack = onehot(iota((CMP_DEV, rows), 0) == bin_row)
    pick = onehot(iota((REC_DEV * n, rows), 0) == rec_row)

    for load in loads[6:]:
        load.wait()
    fwd_high, fwd_low = fwd_high_ref[...], fwd_low_ref[...]
    lane = iota((CMP_DEV, BLOCK), 1)
    turn = (1 - 2 * (iota((CMP_DEV, 2 * BLOCK), 1) % 2)).astype(f32)
    corr[...] = jnp.zeros_like(corr)
    half = LAGS // 2
    before = jnp.zeros((CMP_DEV, half), f32)

    def block_spectrum(pilot, before):
        return mm3(jnp.concatenate([before, pilot[:, :half]], axis=1), fwd_high, fwd_low)

    def add_block(j):
        window = spectra[j] + turn * spectra[j + 1]
        real, imag = window[:, :BLOCK], window[:, BLOCK:]
        wide = jnp.concatenate(
            [real, jnp.where(lane == 0, 0.0, imag), jnp.where(lane == 0, -imag, real)], axis=1
        )
        w = mm(gather_twice, jnp.concatenate(halves(wide), axis=0))
        y = mm3(inbox[:, pl.ds(j * BLOCK, BLOCK)], fwd_high, fwd_low)
        y_real, y_imag = y[:, :BLOCK], y[:, BLOCK:]
        w_real, w_imag, w_other = w[:, :BLOCK], w[:, BLOCK : 2 * BLOCK], w[:, 2 * BLOCK :]
        corr[:, :BLOCK] += y_real * w_real + y_imag * w_imag
        corr[:, BLOCK:] += y_real * w_imag - y_imag * w_other

    for c in range(PARTS):

        @pl.loop(1, n)
        def _(k):
            d = lax.rem(me + (n - k), n)
            trace_copy(c, d, d).wait_recv()

        for j in range(ENDS[c], ENDS[c + 1]):
            high, low = halves(inbox[:, j * BLOCK : (j + 1) * BLOCK])
            pilot = mm(stack, high) + mm(stack, low)
            spectra[j] = block_spectrum(pilot, before)
            before = pilot[:, half:]
            if j > 0:
                add_block(j - 1)
    spectra[blocks] = block_spectrum(jnp.zeros((CMP_DEV, BLOCK), f32), before)
    add_block(blocks - 1)

    lagged = mm3(corr[...], inv_high_ref[...], inv_low_ref[...])
    lag_out[...] = lagged

    @pl.loop(1, n)
    def _(k):
        d = lax.rem(me + k, n)
        lag_copy(d, me).start()

    high, low = halves(lagged)
    rec_out[...] = mm(pick, high) + mm(pick, low)

    for i in range(pairs):
        side_copy(i).start()

    lag_in[mine, :] = lag_out[mine, :]
    for i in range(pairs):
        side_copy(i).wait_recv()
        rec_out[shot_block(i, core), :] += rec_side[i * shot_rows : (i + 1) * shot_rows, :]

    @pl.loop(1, team)
    def _(k):
        rec_copy(lax.rem(rank_in_team + k, team), rank_in_team).start()

    own_rows = pl.ds(pl.multiple_of(rank_in_team * REC_DEV, 8), REC_DEV)
    rec_in[own_rows, :] = rec_out[pl.ds(pl.multiple_of(me * REC_DEV, 8), REC_DEV), :]

    @pl.loop(1, n)
    def _(k):
        d = lax.rem(me + (n - k), n)
        lag_copy(d, d).wait_recv()

    high, low = halves(lag_in[...])
    source_ref[...] = mm(take, high) + mm(take, low)

    @pl.loop(1, team)
    def _(k):
        p = lax.rem(rank_in_team + (team - k), team)
        rec_copy(p, p).wait_recv()

    total = rec_in[0:REC_DEV, :]
    for d in range(1, team):
        total = total + rec_in[d * REC_DEV : (d + 1) * REC_DEV, :]
    received_ref[...] = total

    @pl.loop(1, n)
    def _(k):
        d = lax.rem(me + k, n)
        label_copy(d, me).wait_send()
        for c in range(PARTS):
            trace_copy(c, d, me).wait_send()
        lag_copy(d, me).wait_send()

    for i in range(pairs):
        side_copy(i).wait_send()

    @pl.loop(1, team)
    def _(k):
        rec_copy(lax.rem(rank_in_team + k, team), rank_in_team).wait_send()


def local(n, n_cmp, traces, statics, cmp_owner, cmp_offset, shot_id, receiver_id):
    count, samples = traces.shape
    cap = max(8, 2 * count // n)
    rows = n * cap

    def row(a):
        return a.reshape(1, count)

    tables = [jnp.asarray(t) for t in transform_tables(samples)]
    vmem = pl.BlockSpec(memory_space=pltpu.VMEM)
    return pl.pallas_call(
        functools.partial(kernel, n, n_cmp, cap),
        out_shape=(
            jax.ShapeDtypeStruct((SHOT_DEV, LAGS), f32),
            jax.ShapeDtypeStruct((REC_DEV, LAGS), f32),
        ),
        in_specs=[pl.BlockSpec(memory_space=pltpu.HBM)] * 10,
        out_specs=(vmem, vmem),
        scratch_shapes=[pltpu.VMEM((1, count), jnp.int32) for _ in range(5)]
        + [pltpu.VMEM((count, samples), f32)]
        + [pltpu.VMEM(t.shape, bf16) for t in tables]
        + [
            pltpu.VMEM((2 * count, samples), bf16),
            pltpu.VMEM((rows, samples), f32),
            pltpu.VMEM((rows, samples), f32),
            pltpu.VMEM((n, BLOCK), f32),
            pltpu.VMEM((n, 1, BLOCK), f32),
            pltpu.VMEM((n, 1, BLOCK), f32),
            pltpu.VMEM((samples // BLOCK + 1, CMP_DEV, 2 * BLOCK), f32),
            pltpu.VMEM((rows, 2 * BLOCK), f32),
            pltpu.VMEM((rows, LAGS), f32),
            pltpu.VMEM((rows, LAGS), f32),
            pltpu.VMEM((n * REC_DEV, LAGS), f32),
            pltpu.VMEM((n // 2 * REC_DEV, LAGS), f32),
            pltpu.VMEM((n // 2 * REC_DEV, LAGS), f32),
            pltpu.SemaphoreType.DMA((PARTS + 3, n)),
            pltpu.SemaphoreType.DMA((PARTS + 3, n)),
            pltpu.SemaphoreType.DMA((2, n // n_cmp // 2)),
            pltpu.SemaphoreType.DMA((10,)),
        ],
        compiler_params=pltpu.CompilerParams(
            collective_id=0, has_side_effects=True, vmem_limit_bytes=48 * 1024 * 1024
        ),
    )(row(cmp_owner), row(cmp_offset), row(shot_id), row(receiver_id), row(statics), traces, *tables)


def solution(mesh):
    axes = ("shot", "cmp")
    n = mesh.shape["shot"] * mesh.shape["cmp"]
    return jax.shard_map(
        functools.partial(local, n, mesh.shape["cmp"]),
        mesh=mesh,
        in_specs=(P(axes, None), P(axes), P(axes, None), P(axes), P(axes), P(axes)),
        out_specs=(P(axes, None), P(axes, None)),
        check_vma=False,
    )
```
